32 devices in a mesh: row: 4 (over y, core), col: 8 (over z, x).
Axes of the slice: x: 2, y: 2, z: 4, core: 2. Of those that a mesh axis runs over, the one named last changes fastest.
Arguments:
- factors: float32 [2, 96, 49152], P(None, 'row', 'col'), may hold values from -0.3125 to 0.3125
- covariance: float32 [12288, 12288], P('row', 'col'), may hold values from -26 to 26, as said below
- noise: float32 [12288, 12288], P('row', 'col'), may hold values from -2.4 to 2.4
- positions: float32 [12288], replicated, may hold values from 0 to 1
Outputs:
- forecast: float32 [12288, 12288], P('row', 'col')
The draws below stay inside these ranges and needn't reach their ends.
Inputs may be any that keep to these rules, and one draw needn't show every extreme that they name: covariance is symmetric, with 2 added on its diagonal.
All inputs are finite; a program needn't handle non-finite values.
Results may differ from the reference program's by a relative error of at most 0.00014.
Values sent between devices are 32-bit elements; how exact they have to be, the bound alone decides.
A program may use at most 256 MiB of HBM per device.

```python
import jax
import jax.numpy as jnp
from jax import lax

N = 12288
B = 128
NB = 96


def draw_covariance(key, part):
    first = jax.random.fold_in(key, 0)
    drawn = jax.random.normal(first, (N, N), jnp.float32)
    drawn = jnp.clip(drawn, -6.0, 6.0)
    symmetric = (drawn + drawn.T) * 0.5
    return symmetric + 2.0 * jnp.eye(N, dtype=jnp.float32)


def levels(rng, dims, pieces, least, largest):
    def one(dim, parts):
        steps = jax.random.uniform(jax.random.fold_in(jax.random.fold_in(rng, 6), dim), (parts,), jnp.float32, least / len(pieces), largest / len(pieces))
        return jnp.repeat(jnp.exp(steps), dims[dim] // parts).reshape((-1,) + (1,) * (len(dims) - dim - 1))

    factor_of = one(*pieces[0])
    for cut in pieces[1:]:
        factor_of = factor_of * one(*cut)
    return factor_of


def centred(key, extent, scale, bound, cuts=(), kind=jnp.bfloat16):
    factor_of = levels(key, extent, cuts, -0.22, 0.18) if cuts else 1.0
    drawn = jax.random.normal(key, extent, jnp.float32) * scale * factor_of
    return jnp.minimum(jnp.maximum(drawn, -bound), bound).astype(kind)


def setup_inputs(seed: int = 0) -> dict:
    keys = jax.random.split(jax.random.key(seed), 5)
    factors = centred(keys[0], (2, NB, 3 * B * B), (3 * B) ** -0.5, 0.3125, ((1, 4), (2, 8)), jnp.float32)
    covariance = draw_covariance(jax.random.fold_in(keys[4], 71), 0)
    noise = centred(keys[2], (N, N), 0.3, 2.4, ((0, 4), (1, 8)), jnp.float32)
    positions = jnp.clip(jax.random.uniform(keys[3], (N,), jnp.float32, 0.0, 1.0), 0.0, 1.0)
    return dict(factors=factors, covariance=covariance, noise=noise, positions=positions)


def left_apply(blocks, matrix):
    count = blocks.shape[0]
    size = blocks.shape[2]
    width = matrix.shape[1]
    split = matrix.reshape(count, size, width)
    zero = jnp.zeros((1, size, width), jnp.float32)
    before = jnp.concatenate([zero, split[:-1]], axis=0)
    after = jnp.concatenate([split[1:], zero], axis=0)
    total = jnp.einsum("iab,ibk->iak", blocks[:, 0], before, precision=lax.Precision.HIGHEST)
    total = total + jnp.einsum("iab,ibk->iak", blocks[:, 1], split, precision=lax.Precision.HIGHEST)
    total = total + jnp.einsum("iab,ibk->iak", blocks[:, 2], after, precision=lax.Precision.HIGHEST)
    return total.reshape(count * size, width)


def right_apply(blocks, matrix):
    count = blocks.shape[0]
    size = blocks.shape[2]
    height = matrix.shape[0]
    split = matrix.reshape(height, count, size)
    zero = jnp.zeros((height, 1, size), jnp.float32)
    before = jnp.concatenate([zero, split[:, :-1]], axis=1)
    after = jnp.concatenate([split[:, 1:], zero], axis=1)
    total = jnp.einsum("kib,iab->kia", before, blocks[:, 0], precision=lax.Precision.HIGHEST)
    total = total + jnp.einsum("kib,iab->kia", split, blocks[:, 1], precision=lax.Precision.HIGHEST)
    total = total + jnp.einsum("kib,iab->kia", after, blocks[:, 2], precision=lax.Precision.HIGHEST)
    return total.reshape(height, count * size)


def reference(factors, covariance, noise, positions):
    shaped = factors.reshape(2, NB, 3, B, B)
    moved = left_apply(shaped[0], covariance)
    moved = left_apply(shaped[1], moved)
    spread = right_apply(shaped[0], moved)
    spread = right_apply(shaped[1], spread)
    distance = (positions[:, None] - positions[None, :]) / 0.5
    taper = jnp.exp(-distance * distance)
    return spread * taper + noise
```

```python
import functools

import jax
import jax.numpy as jnp
from jax import lax
from jax.experimental import pallas as pl
from jax.experimental.pallas import tpu as pltpu
from jax.sharding import PartitionSpec as P

B = 128
VMEM = 56 * 1024 * 1024


def parts(x):
    high = x.astype(jnp.bfloat16)
    return high, (x - high.astype(jnp.float32)).astype(jnp.bfloat16)


def dot(a, b):
    return jnp.dot(a, b, preferred_element_type=jnp.float32)


def neighbours(first, last, axis):
    count = lax.axis_size(axis)
    before = lax.ppermute(last, axis, [(i, i + 1) for i in range(count - 1)])
    after = lax.ppermute(first, axis, [(i + 1, i) for i in range(count - 1)])
    return before, after


def compose_kernel(f1, f2, low, high, band, compact, b1h, b1l, b2h, b2l):
    g = pl.program_id(0)
    rows = f1.shape[0]

    @pl.when(g == 0)
    def _():
        for ref in (b1h, b1l, b2h, b2l):
            ref[...] = jnp.zeros_like(ref)

    for r in range(2):
        for k in range(3):
            h, l = parts(f2[2 * g + r, k * B : (k + 1) * B, :])
            at = (slice(r * B, (r + 1) * B), slice((r + k) * B, (r + k + 1) * B))
            b2h[at] = h
            b2l[at] = l
    for j in range(4):
        for k in range(3):
            cut = slice(k * B, (k + 1) * B)
            if j == 0:
                x = jnp.where(g == 0, low[0, cut, :], f1[jnp.maximum(2 * g - 1, 0), cut, :])
            elif j == 3:
                x = jnp.where(
                    g == rows // 2 - 1, high[0, cut, :], f1[jnp.minimum(2 * g + 2, rows - 1), cut, :]
                )
            else:
                x = f1[2 * g + j - 1, cut, :]
            h, l = parts(x)
            at = (slice(j * B, (j + 1) * B), slice((j + k) * B, (j + k + 1) * B))
            b1h[at] = h
            b1l[at] = l
    c = dot(b2h[...], b1h[...]) + dot(b2h[...], b1l[...]) + dot(b2l[...], b1h[...])
    h, l = parts(c)
    band[0, : 2 * B, :] = h
    band[0, 2 * B :, :] = l
    compact[0] = c[:B, : 5 * B]
    compact[1] = c[B:, B:]


def compose(f1, f2, low, high):
    rows = f1.shape[0]
    whole = pl.BlockSpec(f1.shape, lambda g: (0, 0, 0))
    rim = pl.BlockSpec(low.shape, lambda g: (0, 0, 0))
    return pl.pallas_call(
        compose_kernel,
        grid=(rows // 2,),
        in_specs=[whole, whole, rim, rim],
        out_specs=[
            pl.BlockSpec((1, 4 * B, 6 * B), lambda g: (g, 0, 0)),
            pl.BlockSpec((2, B, 5 * B), lambda g: (g, 0, 0)),
        ],
        out_shape=[
            jax.ShapeDtypeStruct((rows // 2, 4 * B, 6 * B), jnp.bfloat16),
            jax.ShapeDtypeStruct((rows, B, 5 * B), jnp.float32),
        ],
        scratch_shapes=[
            pltpu.VMEM((4 * B, 6 * B), jnp.bfloat16),
            pltpu.VMEM((4 * B, 6 * B), jnp.bfloat16),
            pltpu.VMEM((2 * B, 4 * B), jnp.bfloat16),
            pltpu.VMEM((2 * B, 4 * B), jnp.bfloat16),
        ],
        compiler_params=pltpu.CompilerParams(vmem_limit_bytes=VMEM),
        cost_estimate=pl.CostEstimate(
            flops=rows // 2 * 6 * 256 * 512 * 768, bytes_accessed=rows * B * B * 66, transcendentals=0
        ),
        name="compose",
    )(f1, f2, low, high)


def left_kernel(top, own, bottom, band, out, high, low):
    s = pl.program_id(0)
    steps = pl.num_programs(0)
    width = own.shape[1]
    slot = lax.rem(s, 3)

    def keep(ref):
        h, l = parts(ref[...])
        high[slot] = h
        low[slot] = l

    @pl.when(s == 0)
    def _():
        keep(top)

    @pl.when(jnp.logical_and(s > 0, s < steps - 1))
    def _():
        keep(own)

    @pl.when(s == steps - 1)
    def _():
        keep(bottom)

    @pl.when(s >= 2)
    def _():
        step = 2 * B
        for at in range(0, width, step):
            stop = min(at + step, width)
            total = None
            for k in range(3):
                here = lax.rem(s + 1 + k, 3)
                cut = slice(k * 2 * B, (k + 1) * 2 * B)
                x = high[here, :, at:stop]
                both = dot(band[0, :, cut], x)
                term = both[: 2 * B] + both[2 * B :] + dot(band[0, : 2 * B, cut], low[here, :, at:stop])
                total = term if total is None else total + term
            out[:, at:stop] = total


def left(top, own, bottom, band):
    groups = band.shape[0]
    rows, width = own.shape
    rim = pl.BlockSpec((2 * B, width), lambda s: (0, 0))
    return pl.pallas_call(
        left_kernel,
        grid=(groups + 2,),
        in_specs=[
            rim,
            pl.BlockSpec((2 * B, width), lambda s: (jnp.clip(s - 1, 0, groups - 1), 0)),
            rim,
            pl.BlockSpec((1, 4 * B, 6 * B), lambda s: (jnp.maximum(s - 2, 0), 0, 0)),
        ],
        out_specs=pl.BlockSpec((2 * B, width), lambda s: (jnp.maximum(s - 2, 0), 0)),
        out_shape=jax.ShapeDtypeStruct((rows, width), jnp.float32),
        scratch_shapes=[
            pltpu.VMEM((3, 2 * B, width), jnp.bfloat16),
            pltpu.VMEM((3, 2 * B, width), jnp.bfloat16),
        ],
        compiler_params=pltpu.CompilerParams(vmem_limit_bytes=VMEM),
        cost_estimate=pl.CostEstimate(
            flops=6 * rows * 768 * width, bytes_accessed=8 * rows * width, transcendentals=0
        ),
        name="left",
    )(top, own, bottom, band)


def right_kernel(pair, tile, sides, blocks, noise, row_places, col_places, out, bh, bl, th, tl):
    groups = bh.shape[0]
    cols = tile.shape[1]
    span = pair * B

    @pl.when(pl.program_id(0) == 0)
    def _():
        bh[...] = jnp.zeros_like(bh)
        bl[...] = jnp.zeros_like(bl)
        for g in range(groups):
            for r in range(pair):
                h, l = parts(blocks[g * pair + r].T)
                bh[g, r * B : (r + 5) * B, r * B : (r + 1) * B] = h
                bl[g, r * B : (r + 5) * B, r * B : (r + 1) * B] = l

    h, l = parts(sides[:, : 2 * B])
    th[:, : 2 * B] = h
    tl[:, : 2 * B] = l
    h, l = parts(tile[...])
    th[:, 2 * B : 2 * B + cols] = h
    tl[:, 2 * B : 2 * B + cols] = l
    h, l = parts(sides[:, 2 * B :])
    th[:, 2 * B + cols :] = h
    tl[:, 2 * B + cols :] = l
    for g in range(groups):
        cut = slice(g * span, g * span + (pair + 4) * B)
        x = th[:, cut]
        total = dot(x, bh[g]) + dot(tl[:, cut], bh[g]) + dot(x, bl[g])
        here = slice(g * span, (g + 1) * span)
        distance = (row_places[...] - col_places[:, here]) / 0.5
        out[:, here] = total * jnp.exp(-distance * distance) + noise[:, here]


def right(tile, sides, blocks, noise, row_places, col_places):
    rows, cols = tile.shape
    count = cols // B
    pair = 2 if count % 2 == 0 else 1
    height = 512 if rows % 512 == 0 else 256
    band = (count // pair, (pair + 4) * B, pair * B)

    def rowwise(width):
        return pl.BlockSpec((height, width), lambda s: (s, 0))

    return pl.pallas_call(
        functools.partial(right_kernel, pair),
        grid=(rows // height,),
        in_specs=[
            rowwise(cols),
            rowwise(4 * B),
            pl.BlockSpec(blocks.shape, lambda s: (0, 0, 0)),
            rowwise(cols),
            rowwise(1),
            pl.BlockSpec((1, cols), lambda s: (0, 0)),
        ],
        out_specs=rowwise(cols),
        out_shape=jax.ShapeDtypeStruct((rows, cols), jnp.float32),
        scratch_shapes=[
            pltpu.VMEM(band, jnp.bfloat16),
            pltpu.VMEM(band, jnp.bfloat16),
            pltpu.VMEM((height, cols + 4 * B), jnp.bfloat16),
            pltpu.VMEM((height, cols + 4 * B), jnp.bfloat16),
        ],
        compiler_params=pltpu.CompilerParams(vmem_limit_bytes=VMEM),
        cost_estimate=pl.CostEstimate(
            flops=6 * rows * 768 * cols, bytes_accessed=14 * rows * cols, transcendentals=rows * cols
        ),
        name="right",
    )(tile, sides, blocks, noise, row_places, col_places)


def spread(block, owners, owner):
    rows = lax.axis_size("row")
    cols = lax.axis_size("col")
    block = jnp.where(lax.axis_index("row") == owner, block, jnp.zeros_like(block))
    if rows & (rows - 1):
        return lax.psum(block, "row")
    step = rows // 2
    while step:
        pairs = [
            (r * cols + c, (r ^ step) * cols + c)
            for c in range(cols)
            for r in range(rows)
            if (r ^ owners[c]) & (2 * step - 1) == 0
        ]
        block = block + lax.ppermute(block, ("row", "col"), pairs)
        step //= 2
    return block


def body(factors, covariance, noise, positions):
    rows_here, cols_here = covariance.shape
    block_rows = factors.shape[1]
    block_cols = cols_here // B
    cols = lax.axis_size("col")
    col_at = lax.axis_index("col")
    row_at = lax.axis_index("row")
    rim = 2 * B

    shaped = factors.reshape(2, block_rows, factors.shape[2] // B, B)
    gathered = lax.all_gather(shaped, "col", axis=2, tiled=True)

    sides = jnp.concatenate(
        neighbours(covariance[:, :rim], covariance[:, cols_here - rim :], "col"), axis=1
    )
    above, below = neighbours(covariance[:rim], covariance[rows_here - rim :], "row")
    sides_above, sides_below = neighbours(sides[:rim], sides[rows_here - rim :], "row")

    low, high = neighbours(gathered[0, :1], gathered[0, block_rows - 1 :], "row")
    band, compact = compose(gathered[0], gathered[1], low, high)

    owners = [c * block_cols // block_rows for c in range(cols)]
    selected = lax.dynamic_slice_in_dim(compact, col_at * block_cols % block_rows, block_cols, 0)
    matching = spread(selected, owners, col_at * block_cols // block_rows)

    tile = left(above, covariance, below, band)
    tile_sides = left(sides_above, sides, sides_below, band)

    row_places = lax.dynamic_slice_in_dim(positions, row_at * rows_here, rows_here, 0)
    col_places = lax.dynamic_slice_in_dim(positions, col_at * cols_here, cols_here, 0)
    return right(tile, tile_sides, matching, noise, row_places[:, None], col_places[None, :])


def solution(mesh):
    placed = (P(None, "row", "col"), P("row", "col"), P("row", "col"), P())
    return jax.shard_map(
        body, mesh=mesh, in_specs=placed, out_specs=P("row", "col"), check_vma=False
    )
```

```python
import functools

import jax
import jax.numpy as jnp
from jax import lax
from jax.experimental import pallas as pl
from jax.experimental.pallas import tpu as pltpu
from jax.sharding import PartitionSpec as P

B = 128
VMEM = 56 * 1024 * 1024


def parts(x):
    high = x.astype(jnp.bfloat16)
    return high, (x - high.astype(jnp.float32)).astype(jnp.bfloat16)


def dot(a, b):
    return jnp.dot(a, b, preferred_element_type=jnp.float32)


def neighbours(first, last, axis):
    count = lax.axis_size(axis)
    before = lax.ppermute(last, axis, [(i, i + 1) for i in range(count - 1)])
    after = lax.ppermute(first, axis, [(i + 1, i) for i in range(count - 1)])
    return before, after


def compose_kernel(f, low, high, band, compact, b1h, b1l, b2h, b2l):
    g = pl.program_id(0)
    rows = f.shape[1]

    @pl.when(g == 0)
    def _():
        for ref in (b1h, b1l, b2h, b2l):
            ref[...] = jnp.zeros_like(ref)

    for r in range(2):
        for k in range(3):
            h, l = parts(f[1, 2 * g + r, k * B : (k + 1) * B, :])
            at = (slice(r * B, (r + 1) * B), slice((r + k) * B, (r + k + 1) * B))
            b2h[at] = h
            b2l[at] = l
    for j in range(4):
        for k in range(3):
            cut = slice(k * B, (k + 1) * B)
            if j == 0:
                x = jnp.where(g == 0, low[0, cut, :], f[0, jnp.maximum(2 * g - 1, 0), cut, :])
            elif j == 3:
                x = jnp.where(
                    g == rows // 2 - 1, high[0, cut, :], f[0, jnp.minimum(2 * g + 2, rows - 1), cut, :]
                )
            else:
                x = f[0, 2 * g + j - 1, cut, :]
            h, l = parts(x)
            at = (slice(j * B, (j + 1) * B), slice((j + k) * B, (j + k + 1) * B))
            b1h[at] = h
            b1l[at] = l
    c = dot(b2h[...], b1h[...]) + dot(b2h[...], b1l[...]) + dot(b2l[...], b1h[...])
    h, l = parts(c)
    band[0, : 2 * B, :] = h
    band[0, 2 * B :, :] = l
    compact[0] = c[:B, : 5 * B]
    compact[1] = c[B:, B:]


def compose(f, low, high):
    rows = f.shape[1]
    whole = pl.BlockSpec(f.shape, lambda g: (0, 0, 0, 0))
    rim = pl.BlockSpec(low.shape, lambda g: (0, 0, 0))
    return pl.pallas_call(
        compose_kernel,
        grid=(rows // 2,),
        in_specs=[whole, rim, rim],
        out_specs=[
            pl.BlockSpec((1, 4 * B, 6 * B), lambda g: (g, 0, 0)),
            pl.BlockSpec((2, B, 5 * B), lambda g: (g, 0, 0)),
        ],
        out_shape=[
            jax.ShapeDtypeStruct((rows // 2, 4 * B, 6 * B), jnp.bfloat16),
            jax.ShapeDtypeStruct((rows, B, 5 * B), jnp.float32),
        ],
        scratch_shapes=[
            pltpu.VMEM((4 * B, 6 * B), jnp.bfloat16),
            pltpu.VMEM((4 * B, 6 * B), jnp.bfloat16),
            pltpu.VMEM((2 * B, 4 * B), jnp.bfloat16),
            pltpu.VMEM((2 * B, 4 * B), jnp.bfloat16),
        ],
        compiler_params=pltpu.CompilerParams(vmem_limit_bytes=VMEM),
        cost_estimate=pl.CostEstimate(
            flops=rows * B * B, bytes_accessed=rows * B * B, transcendentals=0
        ),
        name="compose",
    )(f, low, high)


def left_kernel(top, own, bottom, band, out, high, low):
    s = pl.program_id(0)
    steps = pl.num_programs(0)
    width = own.shape[1]
    slot = lax.rem(s, 3)

    def keep(ref):
        h, l = parts(ref[...])
        high[slot] = h
        low[slot] = l

    @pl.when(s == 0)
    def _():
        keep(top)

    @pl.when(jnp.logical_and(s > 0, s < steps - 1))
    def _():
        keep(own)

    @pl.when(s == steps - 1)
    def _():
        keep(bottom)

    @pl.when(s >= 2)
    def _():
        step = 2 * B
        for at in range(0, width, step):
            stop = min(at + step, width)
            total = None
            for k in range(3):
                here = lax.rem(s + 1 + k, 3)
                cut = slice(k * 2 * B, (k + 1) * 2 * B)
                x = high[here, :, at:stop]
                both = dot(band[0, :, cut], x)
                term = both[: 2 * B] + both[2 * B :] + dot(band[0, : 2 * B, cut], low[here, :, at:stop])
                total = term if total is None else total + term
            out[:, at:stop] = total


def left(top, own, bottom, band):
    groups = band.shape[0]
    rows, width = own.shape
    rim = pl.BlockSpec((2 * B, width), lambda s: (0, 0))
    return pl.pallas_call(
        left_kernel,
        grid=(groups + 2,),
        in_specs=[
            rim,
            pl.BlockSpec((2 * B, width), lambda s: (jnp.clip(s - 1, 0, groups - 1), 0)),
            rim,
            pl.BlockSpec((1, 4 * B, 6 * B), lambda s: (jnp.maximum(s - 2, 0), 0, 0)),
        ],
        out_specs=pl.BlockSpec((2 * B, width), lambda s: (jnp.maximum(s - 2, 0), 0)),
        out_shape=jax.ShapeDtypeStruct((rows, width), jnp.float32),
        scratch_shapes=[
            pltpu.VMEM((3, 2 * B, width), jnp.bfloat16),
            pltpu.VMEM((3, 2 * B, width), jnp.bfloat16),
        ],
        compiler_params=pltpu.CompilerParams(vmem_limit_bytes=VMEM),
        cost_estimate=pl.CostEstimate(
            flops=rows * width, bytes_accessed=rows * width, transcendentals=0
        ),
        name="left",
    )(top, own, bottom, band)


def right_kernel(pair, tile, sides, held, came, noise, row_places, col_places, out, bh, bl, th, tl):
    groups = bh.shape[0]
    cols = tile.shape[1]
    span = pair * B

    @pl.when(pl.program_id(0) == 0)
    def _():
        bh[...] = jnp.zeros_like(bh)
        bl[...] = jnp.zeros_like(bl)
        for g in range(groups):
            for r in range(pair):
                h, l = parts((held[g * pair + r] + came[g * pair + r]).T)
                bh[g, r * B : (r + 5) * B, r * B : (r + 1) * B] = h
                bl[g, r * B : (r + 5) * B, r * B : (r + 1) * B] = l

    h, l = parts(sides[:, : 2 * B])
    th[:, : 2 * B] = h
    tl[:, : 2 * B] = l
    h, l = parts(tile[...])
    th[:, 2 * B : 2 * B + cols] = h
    tl[:, 2 * B : 2 * B + cols] = l
    h, l = parts(sides[:, 2 * B :])
    th[:, 2 * B + cols :] = h
    tl[:, 2 * B + cols :] = l
    for g in range(groups):
        cut = slice(g * span, g * span + (pair + 4) * B)
        x = th[:, cut]
        total = dot(x, bh[g]) + dot(tl[:, cut], bh[g]) + dot(x, bl[g])
        here = slice(g * span, (g + 1) * span)
        distance = (row_places[...] - col_places[:, here]) / 0.5
        out[:, here] = total * jnp.exp(-distance * distance) + noise[:, here]


def right(tile, sides, held, came, noise, row_places, col_places):
    rows, cols = tile.shape
    count = cols // B
    pair = 2 if count % 2 == 0 else 1
    height = 512 if rows % 512 == 0 else 256
    band = (count // pair, (pair + 4) * B, pair * B)

    def rowwise(width):
        return pl.BlockSpec((height, width), lambda s: (s, 0))

    return pl.pallas_call(
        functools.partial(right_kernel, pair),
        grid=(rows // height,),
        in_specs=[
            rowwise(cols),
            rowwise(4 * B),
            pl.BlockSpec(held.shape, lambda s: (0, 0, 0)),
            pl.BlockSpec(held.shape, lambda s: (0, 0, 0)),
            rowwise(cols),
            rowwise(1),
            pl.BlockSpec((1, cols), lambda s: (0, 0)),
        ],
        out_specs=rowwise(cols),
        out_shape=jax.ShapeDtypeStruct((rows, cols), jnp.float32),
        scratch_shapes=[
            pltpu.VMEM(band, jnp.bfloat16),
            pltpu.VMEM(band, jnp.bfloat16),
            pltpu.VMEM((height, cols + 4 * B), jnp.bfloat16),
            pltpu.VMEM((height, cols + 4 * B), jnp.bfloat16),
        ],
        compiler_params=pltpu.CompilerParams(vmem_limit_bytes=VMEM),
        cost_estimate=pl.CostEstimate(
            flops=6 * rows * 768 * cols, bytes_accessed=14 * rows * cols, transcendentals=rows * cols
        ),
        name="right",
    )(tile, sides, held, came, noise, row_places, col_places)


def spread(block, owners, owner, meanwhile):
    rows = lax.axis_size("row")
    cols = lax.axis_size("col")
    block = jnp.where(lax.axis_index("row") == owner, block, jnp.zeros_like(block))
    if rows & (rows - 1):
        return lax.psum(block, "row"), jnp.zeros_like(block), meanwhile
    came = jnp.zeros_like(block)
    step = rows // 2
    while step:
        if step == rows // 4:
            came, meanwhile = lax.optimization_barrier((came, meanwhile))
        block = block + came
        pairs = [
            (r * cols + c, (r ^ step) * cols + c)
            for c in range(cols)
            for r in range(rows)
            if (r ^ owners[c]) & (2 * step - 1) == 0
        ]
        came = lax.ppermute(block, ("row", "col"), pairs)
        step //= 2
    return block, came, meanwhile


def body(factors, covariance, noise, positions):
    rows_here, cols_here = covariance.shape
    block_rows = factors.shape[1]
    block_cols = cols_here // B
    cols = lax.axis_size("col")
    col_at = lax.axis_index("col")
    row_at = lax.axis_index("row")
    rim = 2 * B

    shaped = factors.reshape(2, block_rows, factors.shape[2] // B, B)
    gathered = lax.all_gather(shaped, "col", axis=2, tiled=True)

    cut = rows_here // 2
    first, last = covariance[:, :rim], covariance[:, cols_here - rim :]
    before, after = neighbours(first[:cut], last[:cut], "col")
    above, below = neighbours(covariance[:rim], covariance[rows_here - rim :], "row")
    gathered, before, after, above, below, first, last = lax.optimization_barrier(
        (gathered, before, after, above, below, first[cut:], last[cut:])
    )
    late_before, late_after = neighbours(first, last, "col")
    low, high = neighbours(gathered[0, :1], gathered[0, block_rows - 1 :], "row")
    band, compact = compose(gathered, low, high)

    owners = [c * block_cols // block_rows for c in range(cols)]
    selected = lax.dynamic_slice_in_dim(compact, col_at * block_cols % block_rows, block_cols, 0)

    tile = left(above, covariance, below, band)
    held, came, (tile, late_before, late_after) = spread(
        selected,
        owners,
        col_at * block_cols // block_rows,
        (tile, late_before, late_after),
    )
    sides = jnp.concatenate(
        [
            jnp.concatenate([before, after], axis=1),
            jnp.concatenate([late_before, late_after], axis=1),
        ],
        axis=0,
    )
    sides_above, sides_below = neighbours(sides[:rim], sides[rows_here - rim :], "row")
    tile_sides = left(sides_above, sides, sides_below, band)

    row_places = lax.dynamic_slice_in_dim(positions, row_at * rows_here, rows_here, 0)
    col_places = lax.dynamic_slice_in_dim(positions, col_at * cols_here, cols_here, 0)
    return right(tile, tile_sides, held, came, noise, row_places[:, None], col_places[None, :])


def solution(mesh):
    placed = (P(None, "row", "col"), P("row", "col"), P("row", "col"), P())
    return jax.shard_map(
        body, mesh=mesh, in_specs=placed, out_specs=P("row", "col"), check_vma=False
    )
```
